32 devices in a mesh: ctx: 8 (over z, x), head: 4 (over y, core).
Axes of the slice: x: 2, y: 2, z: 4, core: 2. Of those that a mesh axis runs over, the one named last changes fastest.
Arguments:
- queries: bfloat16 [16, 256, 5120], P('head', 'ctx'), may hold values from -32 to 32
- keys: bfloat16 [16, 256, 5120], P('head', 'ctx'), may hold values from -32 to 32
- values: bfloat16 [16, 256, 5120], P('head', 'ctx'), may hold values from -6 to 6
- out_grad: bfloat16 [16, 256, 5120], P('head', 'ctx'), may hold values from -6 to 6
- band_frames: int32 [16, 8, 8], P(None, 'ctx'), may hold values from -1 to 15, as said below
- frame_order: int32 [16], replicated, may hold values from 0 to 15, each once
Outputs:
- attended: bfloat16 [16, 256, 5120], P('head', 'ctx')
- query_grad: bfloat16 [16, 256, 5120], P('head', 'ctx')
- key_grad: bfloat16 [16, 256, 5120], P('head', 'ctx')
- value_grad: bfloat16 [16, 256, 5120], P('head', 'ctx')
The draws below stay inside these ranges and needn't reach their ends.
Inputs may be any that keep to these rules, and one draw needn't show every extreme that they name: `band_frames`: entry [f, c, 2 b + r] is f - d for r = 0 or f + d for r = 1, with 2**b <= d < 2**(b+1), or -1 where that frame lies outside 0 to 15. `frame_order`: each frame once.
All inputs are finite; a program needn't handle non-finite values.
Results may differ from the reference program's by a relative error of at most 0.012.
Values may be sent and summed in bfloat16 or wider, within the bound.
A program may use at most 192 MiB of HBM per device.

```python
import jax
import jax.numpy as jnp
from jax import lax

HEADS = 40
HD = 128
FRAMES = 16
NBAND = 8
SLAB = 32
SLABS = 8
SPATIAL = 256


def draw_queries(key, part):
    key = jax.random.fold_in(key, 1)
    drawn = jax.random.normal(key, (FRAMES, SLAB * SLABS, HEADS * HD), jnp.float32)
    return drawn.astype(jnp.bfloat16)


def draw_keys(key, part):
    key = jax.random.fold_in(key, 2)
    drawn = jax.random.normal(key, (FRAMES, SLAB * SLABS, HEADS * HD), jnp.float32)
    return drawn.astype(jnp.bfloat16)


def draw_band_frames(key, part):
    key = jax.random.fold_in(key, 7)
    slot_index = jnp.arange(NBAND, dtype=jnp.int32)
    band_start = jnp.left_shift(jnp.int32(1), slot_index // 2)
    jitter = jax.random.randint(key, (FRAMES, SLABS, NBAND), 0, 1 << 30, dtype=jnp.int32) % band_start[None, None, :]
    distance = band_start[None, None, :] + jitter
    frame_index = jnp.arange(FRAMES, dtype=jnp.int32)[:, None, None]
    key_frame = jnp.where(slot_index[None, None, :] % 2 == 0, frame_index - distance, frame_index + distance)
    return jnp.where((key_frame >= 0) & (key_frame < FRAMES), key_frame, -1).astype(jnp.int32)


def level_of(key, dims, cuts, low, largest):
    loudness, own = 1.0, jax.random.fold_in(key, 6)
    for dim, parts in cuts:
        draws = jnp.exp(jax.random.uniform(jax.random.fold_in(own, dim), (parts,), jnp.float32, low / len(cuts), largest / len(cuts)))
        loudness = loudness * jnp.repeat(draws, dims[dim] // parts).reshape([-1 if axis == dim else 1 for axis in range(len(dims))])
    return loudness


def normal_values(stream_key, dims, scale, most, cuts=(), held_as=jnp.bfloat16):
    loudness = level_of(stream_key, dims, cuts, -0.22, 0.18) if cuts else 1.0
    entries = jax.random.normal(stream_key, dims, jnp.float32) * scale * loudness
    return jnp.minimum(jnp.maximum(entries, -most), most).astype(held_as)


def setup_inputs(seed: int = 0) -> dict:
    key_of = jax.random.split(jax.random.key(seed), 7)
    return {
        "queries": draw_queries(jax.random.fold_in(key_of[6], 71), 0),
        "keys": draw_keys(jax.random.fold_in(key_of[6], 71), 0),
        "values": normal_values(key_of[2], (FRAMES, SPATIAL, HEADS * HD), 1.0, 6.0, ((0, 4), (1, 8))),
        "out_grad": normal_values(key_of[3], (FRAMES, SPATIAL, HEADS * HD), 1.0, 6.0, ((0, 4), (1, 8))),
        "band_frames": draw_band_frames(jax.random.fold_in(key_of[6], 71), 0),
        "frame_order": jax.random.permutation(key_of[5], FRAMES).astype(jnp.int32),
    }


NEGATIVE = -1e30
GROUP = 4


def far_positions(slot_frames, frame_order):
    count = frame_order.shape[0]
    frame_ids = jnp.arange(count, dtype=jnp.int32)
    one_hot = (frame_order[:, None] == frame_ids[None, :]).astype(jnp.int32)
    inverse = jnp.sum(one_hot * frame_ids[:, None], axis=0)
    picked = jnp.sum(one_hot[:, :, None] * slot_frames[None, :, :], axis=1)
    far_rows = jnp.sum((picked[:, :, None] == frame_ids[None, None, :]).astype(jnp.int32) * inverse[None, None, :], axis=2)
    return far_rows.astype(jnp.int32), picked >= 0


def attend(query_block, key_block, value_block, key_mask, grad_block, score_scale):
    query_f = query_block.astype(jnp.float32)
    key_f = key_block.astype(jnp.float32)
    value_f = value_block.astype(jnp.float32)
    grad_f = grad_block.astype(jnp.float32)
    scores = jnp.einsum("gqhd,gkhd->ghqk", query_f, key_f) * score_scale
    scores = jnp.where(key_mask[:, None, None, :], scores, NEGATIVE)
    highest = jnp.max(scores, axis=-1, keepdims=True)
    log_total = highest + jnp.log(jnp.sum(jnp.exp(scores - highest), axis=-1, keepdims=True))
    softmax = jnp.exp(scores - log_total)
    weights = lax.optimization_barrier(softmax.astype(jnp.bfloat16)).astype(jnp.float32)
    attended = lax.optimization_barrier(jnp.einsum("ghqk,gkhd->gqhd", weights, value_f).astype(jnp.bfloat16))
    row_delta = jnp.sum(grad_f * attended.astype(jnp.float32), axis=-1)
    prob_grads = jnp.einsum("gqhd,gkhd->ghqk", grad_f, value_f)
    score_grads = softmax * (prob_grads - jnp.transpose(row_delta, (0, 2, 1))[..., None]) * score_scale
    score_grads = lax.optimization_barrier(score_grads.astype(jnp.bfloat16)).astype(jnp.float32)
    query_grad = jnp.einsum("ghqk,gkhd->gqhd", score_grads, key_f).astype(jnp.bfloat16)
    key_grad = jnp.einsum("ghqk,gqhd->gkhd", score_grads, query_f)
    value_grad = jnp.einsum("ghqk,gqhd->gkhd", weights, grad_f)
    return attended, query_grad, key_grad, value_grad


def reference(queries, keys, values, out_grad, band_frames, frame_order):
    rim_rows = SLAB
    span_rows = SLAB + 2 * rim_rows
    columns = HEADS * HD
    score_scale = HD ** -0.5
    total_rows = SLAB * SLABS
    padded_keys = jnp.pad(keys, ((0, 0), (rim_rows, rim_rows), (0, 0)))
    padded_values = jnp.pad(values, ((0, 0), (rim_rows, rim_rows), (0, 0)))
    four_dims = (GROUP, -1, HEADS, HD)

    def slab_pass(slab_index):
        offset = slab_index * SLAB
        position = offset - rim_rows + jnp.arange(span_rows, dtype=jnp.int32)
        window_valid = (position >= 0) & (position < total_rows)
        query_slab = lax.dynamic_slice_in_dim(queries, offset, SLAB, 1)
        key_slab = lax.dynamic_slice_in_dim(keys, offset, SLAB, 1)
        value_slab = lax.dynamic_slice_in_dim(values, offset, SLAB, 1)
        grad_slab = lax.dynamic_slice_in_dim(out_grad, offset, SLAB, 1)
        key_window = lax.dynamic_slice_in_dim(padded_keys, offset, span_rows, 1)
        value_window = lax.dynamic_slice_in_dim(padded_values, offset, span_rows, 1)
        slot_frames = lax.dynamic_index_in_dim(band_frames, slab_index, 1, keepdims=False)
        far_rows, far_valid = far_positions(slot_frames, frame_order)

        def group_step(carry, group_index):
            window_sum, far_sum = carry
            start_frame = group_index * GROUP

            def pick_rows(source):
                return lax.dynamic_slice_in_dim(source, start_frame, GROUP, 0)

            rows_here = pick_rows(far_rows)
            valid_here = pick_rows(far_valid)
            key_block = jnp.concatenate((pick_rows(key_window), key_slab[rows_here].reshape(GROUP, NBAND * SLAB, columns)), axis=1)
            value_block = jnp.concatenate((pick_rows(value_window), value_slab[rows_here].reshape(GROUP, NBAND * SLAB, columns)), axis=1)
            key_mask = jnp.concatenate((jnp.broadcast_to(window_valid[None, :], (GROUP, span_rows)), jnp.repeat(valid_here, SLAB, axis=1)), axis=1)
            attended, query_grad, key_grad, value_grad = attend(pick_rows(query_slab).reshape(four_dims), key_block.reshape(four_dims), value_block.reshape(four_dims), key_mask, pick_rows(grad_slab).reshape(four_dims), score_scale)
            key_terms = jnp.stack((key_grad, value_grad)).reshape(2, GROUP, span_rows + NBAND * SLAB, columns)
            window_sum = lax.dynamic_update_slice_in_dim(window_sum, key_terms[:, :, :span_rows], start_frame, 1)
            far_sum = far_sum.at[:, rows_here.reshape(-1)].add(key_terms[:, :, span_rows:].reshape(2, GROUP * NBAND, SLAB, columns))
            return (window_sum, far_sum), (attended.reshape(GROUP, SLAB, columns), query_grad.reshape(GROUP, SLAB, columns))

        start = (jnp.zeros((2, FRAMES, span_rows, columns), jnp.float32), jnp.zeros((2, FRAMES, SLAB, columns), jnp.float32))
        (window_sum, far_sum), (attended, query_grad) = lax.scan(group_step, start, jnp.arange(FRAMES // GROUP, dtype=jnp.int32))
        center = window_sum[:, :, rim_rows:rim_rows + SLAB] + far_sum
        lower_rim = window_sum[:, :, :rim_rows].astype(jnp.bfloat16)
        upper_rim = window_sum[:, :, rim_rows + SLAB:].astype(jnp.bfloat16)
        return attended.reshape(FRAMES, SLAB, columns), query_grad.reshape(FRAMES, SLAB, columns), center, lower_rim, upper_rim

    attended, query_grad, center, lower_rim, upper_rim = lax.map(slab_pass, jnp.arange(SLABS, dtype=jnp.int32))
    zeros_rim = jnp.zeros_like(lower_rim[:1])
    from_above = jnp.concatenate((lower_rim[1:], zeros_rim), axis=0).astype(jnp.float32)
    from_below = jnp.concatenate((zeros_rim, upper_rim[:-1]), axis=0).astype(jnp.float32)
    center = center.at[:, :, :, SLAB - rim_rows:].add(from_above)
    center = center.at[:, :, :, :rim_rows].add(from_below)
    gradients = center.astype(jnp.bfloat16)

    def to_frames(source):
        return jnp.transpose(source, (1, 0, 2, 3)).reshape(FRAMES, total_rows, columns)

    return to_frames(attended), to_frames(query_grad), to_frames(gradients[:, 0]), to_frames(gradients[:, 1])
```

```python
import functools
import math

import jax
import jax.numpy as jnp
from jax import lax
from jax.experimental import pallas as pl
from jax.experimental.pallas import tpu as pltpu
from jax.sharding import PartitionSpec as P

HD = 128
NEGATIVE = -1e30
MESH = pl.DeviceIdType.MESH
LANES = 128


def nt(a, b):
    return lax.dot_general(a, b, (((1,), (1,)), ((), ())), preferred_element_type=jnp.float32)


def nn(a, b):
    return jnp.dot(a, b, preferred_element_type=jnp.float32)


def kernel(
    dims,
    q_ref,
    k_ref,
    v_ref,
    g_ref,
    bias_ref,
    o_ref,
    dq_ref,
    dk_ref,
    dv_ref,
    buf,
    halo,
    obuf,
    gsend,
    grecv,
    acc,
    bias_buf,
    bias_full,
    prob_t,
    grad_t,
    in_send,
    in_recv,
    out_send,
    out_recv,
    halo_send,
    halo_recv,
    gh_send,
    gh_recv,
    bias_send,
    bias_recv,
):
    groups, merge, ranks, local_heads, frames, part, slab = dims
    members = merge * ranks
    length = frames * slab
    per_chunk = LANES // slab
    scale = HD ** (-0.5)
    log_scale = scale * math.log2(math.e)

    ctx = lax.axis_index("ctx")
    rank = lax.axis_index("head")
    group = lax.div(ctx, merge)
    inner = lax.rem(ctx, merge)
    me = inner * ranks + rank
    has_prev = group > 0
    has_next = group < groups - 1
    prev_id = (ctx - merge, rank)
    next_id = (ctx + merge, rank)

    def member(step):
        slot = lax.rem(me + step, members)
        return slot, (group * merge + lax.div(slot, ranks), lax.rem(slot, ranks))

    barrier = pltpu.get_barrier_semaphore()
    for step in range(1, members):
        pl.semaphore_signal(barrier, inc=1, device_id=member(step)[1], device_id_type=MESH)

    @pl.when(has_prev)
    def _():
        pl.semaphore_signal(barrier, inc=1, device_id=prev_id, device_id_type=MESH)

    @pl.when(has_next)
    def _():
        pl.semaphore_signal(barrier, inc=1, device_id=next_id, device_id_type=MESH)

    @pl.when(jnp.logical_not(has_prev))
    def _():
        halo[:, 0] = jnp.zeros(halo.shape[:1] + halo.shape[2:], halo.dtype)

    @pl.when(jnp.logical_not(has_next))
    def _():
        halo[:, 1] = jnp.zeros(halo.shape[:1] + halo.shape[2:], halo.dtype)

    pl.semaphore_wait(
        barrier, members - 1 + has_prev.astype(jnp.int32) + has_next.astype(jnp.int32)
    )

    def bias_copy(step):
        other = lax.rem(inner + step, merge)
        return pltpu.make_async_remote_copy(
            src_ref=bias_ref,
            dst_ref=bias_buf.at[inner],
            send_sem=bias_send.at[step],
            recv_sem=bias_recv.at[step],
            device_id=(group * merge + other, rank),
            device_id_type=MESH,
        )

    for step in range(1, merge):
        bias_copy(step).start()

    mine = pl.ds(me * part, part)

    @pl.loop(0, local_heads)
    def _(h):
        for step in list(range(1, members)) + [0]:
            slot, device = member(step)
            columns = pl.ds(pl.multiple_of((slot * local_heads + h) * HD, HD), HD)
            for a, source in ((1, k_ref), (2, v_ref), (0, q_ref), (3, g_ref)):
                src, dst = source.at[:, :, columns], buf.at[h, a, mine]
                if step:
                    pltpu.make_async_remote_copy(
                        src_ref=src,
                        dst_ref=dst,
                        send_sem=in_send,
                        recv_sem=in_recv.at[h],
                        device_id=device,
                        device_id_type=MESH,
                    ).start()
                else:
                    pltpu.make_async_copy(src, dst, in_recv.at[h]).start()

    bias_buf[inner] = bias_ref[...]
    for step in range(1, merge):
        bias_copy(step).wait()
    for s in range(merge):
        for frame in range(frames):
            bias_full[s, frame * slab : (frame + 1) * slab, :] = jnp.broadcast_to(
                bias_buf[s, frame : frame + 1, :], (slab, length)
            )

    last = (merge - 1) * frames

    def arrive(h):
        pltpu.make_async_copy(buf.at[h], buf.at[h], in_recv.at[h]).wait()

        @pl.when(has_next)
        def _():
            pltpu.make_async_remote_copy(
                src_ref=buf.at[h, pl.ds(1, 2), pl.ds(last, frames)],
                dst_ref=halo.at[h, 0],
                send_sem=halo_send.at[0],
                recv_sem=halo_recv.at[h, 0],
                device_id=next_id,
                device_id_type=MESH,
            ).start()

        @pl.when(has_prev)
        def _():
            pltpu.make_async_remote_copy(
                src_ref=buf.at[h, pl.ds(1, 2), pl.ds(0, frames)],
                dst_ref=halo.at[h, 1],
                send_sem=halo_send.at[1],
                recv_sem=halo_recv.at[h, 1],
                device_id=prev_id,
                device_id_type=MESH,
            ).start()

    def send_out(h, arrays):
        columns = pl.ds(pl.multiple_of((me * local_heads + h) * HD, HD), HD)
        for step in list(range(1, members)) + [0]:
            slot, device = member(step)
            for a, target in arrays:
                src, dst = obuf.at[h, a, pl.ds(slot * part, part)], target.at[:, :, columns]
                if step:
                    pltpu.make_async_remote_copy(
                        src_ref=src,
                        dst_ref=dst,
                        send_sem=out_send,
                        recv_sem=out_recv.at[a],
                        device_id=device,
                        device_id_type=MESH,
                    ).start()
                else:
                    pltpu.make_async_copy(src, dst, out_recv.at[a]).start()

    lane_frame = lax.div(lax.broadcasted_iota(jnp.int32, (slab, LANES), 1), slab)

    def compact(block):
        result = block[:slab]
        for i in range(1, per_chunk):
            result = jnp.where(lane_frame == i, block[i * slab : (i + 1) * slab], result)
        return result

    def expand(block):
        return jnp.concatenate(
            [jnp.where(lane_frame == i, block, 0.0) for i in range(per_chunk)], axis=0
        ).astype(jnp.bfloat16)

    def compute(h):
        @pl.when(has_prev)
        def _():
            pltpu.make_async_copy(halo.at[h, 0], halo.at[h, 0], halo_recv.at[h, 0]).wait()

        @pl.when(has_next)
        def _():
            pltpu.make_async_copy(halo.at[h, 1], halo.at[h, 1], halo_recv.at[h, 1]).wait()

        edge_prev = jnp.where(has_prev, 0.0, NEGATIVE)
        edge_next = jnp.where(has_next, 0.0, NEGATIVE)

        def rows_of(a, s):
            return buf[h, a, s * frames : (s + 1) * frames].reshape(length, HD)

        keys = [halo[h, 0, 0].reshape(length, HD)]
        values = [halo[h, 0, 1].reshape(length, HD)]
        for s in range(merge):
            keys.append(rows_of(1, s))
            values.append(rows_of(2, s))
        keys.append(halo[h, 1, 0].reshape(length, HD))
        values.append(halo[h, 1, 1].reshape(length, HD))
        keys_t = [x.T for x in keys]
        values_t = [x.T for x in values]

        acc[h] = jnp.zeros(acc.shape[1:], acc.dtype)

        def add_term(a, s, at, term):
            if s < 0 or s >= merge:
                side = 0 if s < 0 else 1
                first = at // slab
                gsend[h, side, a, first : first + per_chunk] = term.astype(jnp.bfloat16).reshape(
                    per_chunk, slab, HD
                )
            else:
                start = s * length + at
                acc[h, a, start : start + LANES] += term

        for s in range(merge):
            query, grad = rows_of(0, s), rows_of(3, s)
            own_k, own_v = keys[s + 1], values[s + 1]
            for at in range(0, length, LANES):
                rows = slice(at, at + LANES)
                q, g = query[rows], grad[rows]
                score = nt(own_k, q) * log_scale + bias_full[s, :, rows]
                score_p = compact(nt(keys[s][rows], q)) * log_scale
                score_n = compact(nt(keys[s + 2][rows], q)) * log_scale
                if s == 0:
                    score_p = score_p + edge_prev
                if s == merge - 1:
                    score_n = score_n + edge_next
                sides = jnp.maximum(score_p, score_n)
                top = jnp.maximum(
                    jnp.max(score, axis=0, keepdims=True), jnp.max(sides, axis=0, keepdims=True)
                )
                e, e_p, e_n = jnp.exp2(score - top), jnp.exp2(score_p - top), jnp.exp2(score_n - top)
                total = jnp.sum(e, axis=0, keepdims=True) + jnp.sum(
                    e_p + e_n, axis=0, keepdims=True
                )
                d = nt(own_v, g)
                d_p = compact(nt(values[s][rows], g))
                d_n = compact(nt(values[s + 2][rows], g))
                inv = 1.0 / total
                delta = inv * (
                    jnp.sum(e * d, axis=0, keepdims=True)
                    + jnp.sum(e_p * d_p + e_n * d_n, axis=0, keepdims=True)
                )
                inv_scale = inv * scale
                p = (e * inv).astype(jnp.bfloat16)
                ds = ((e * inv_scale) * (d - delta)).astype(jnp.bfloat16)
                p_p, p_n = expand(e_p * inv), expand(e_n * inv)
                ds_p = expand((e_p * inv_scale) * (d_p - delta))
                ds_n = expand((e_n * inv_scale) * (d_n - delta))
                prob_t[:, rows] = p
                grad_t[:, rows] = ds
                out_t = (
                    nn(values_t[s + 1], p)
                    + nn(values_t[s][:, rows], p_p)
                    + nn(values_t[s + 2][:, rows], p_n)
                )
                dq_t = (
                    nn(keys_t[s + 1], ds)
                    + nn(keys_t[s][:, rows], ds_p)
                    + nn(keys_t[s + 2][:, rows], ds_n)
                )
                first = s * frames + at // slab
                put = slice(first, first + per_chunk)
                obuf[h, 0, put] = out_t.T.astype(jnp.bfloat16).reshape(per_chunk, slab, HD)
                obuf[h, 1, put] = dq_t.T.astype(jnp.bfloat16).reshape(per_chunk, slab, HD)
                add_term(0, s - 1, at, nn(ds_p, q))
                add_term(1, s - 1, at, nn(p_p, g))
                add_term(0, s + 1, at, nn(ds_n, q))
                add_term(1, s + 1, at, nn(p_n, g))
            whole = slice(s * length, (s + 1) * length)
            acc[h, 0, whole] += nn(grad_t[...], query)
            acc[h, 1, whole] += nn(prob_t[...], grad)

        @pl.when(has_prev)
        def _():
            pltpu.make_async_remote_copy(
                src_ref=gsend.at[h, 0],
                dst_ref=grecv.at[h, 1],
                send_sem=gh_send.at[0],
                recv_sem=gh_recv.at[h, 1],
                device_id=prev_id,
                device_id_type=MESH,
            ).start()

        @pl.when(has_next)
        def _():
            pltpu.make_async_remote_copy(
                src_ref=gsend.at[h, 1],
                dst_ref=grecv.at[h, 0],
                send_sem=gh_send.at[1],
                recv_sem=gh_recv.at[h, 0],
                device_id=next_id,
                device_id_type=MESH,
            ).start()

        send_out(h, ((0, o_ref), (1, dq_ref)))

    def finish(h):
        for side, present, s in ((0, has_prev, 0), (1, has_next, merge - 1)):

            @pl.when(present)
            def _():
                pltpu.make_async_copy(
                    grecv.at[h, side], grecv.at[h, side], gh_recv.at[h, side]
                ).wait()
                term = grecv[h, side].astype(jnp.float32).reshape(2, length, HD)
                acc[h, :, s * length : (s + 1) * length] += term

        obuf[h, 2:4] = acc[h].astype(jnp.bfloat16).reshape(2, merge * frames, slab, HD)
        send_out(h, ((2, dk_ref), (3, dv_ref)))

    arrive(0)

    @pl.loop(0, local_heads)
    def _(h):
        @pl.when(h < local_heads - 1)
        def _():
            arrive(h + 1)

        compute(h)

        @pl.when(h > 0)
        def _():
            finish(h - 1)

    finish(local_heads - 1)

    sent = pl.ds(0, (members - 1) * part)
    pltpu.make_async_copy(buf.at[:, :, sent], buf.at[:, :, sent], in_send).wait()
    pltpu.make_async_copy(obuf.at[:, :, sent], obuf.at[:, :, sent], out_send).wait()
    for a, target in enumerate((o_ref, dq_ref, dk_ref, dv_ref)):
        pltpu.make_async_copy(target, target, out_recv.at[a]).wait()

    @pl.when(has_next)
    def _():
        pltpu.make_async_copy(halo.at[:, 0], halo.at[:, 0], halo_send.at[0]).wait()
        pltpu.make_async_copy(gsend.at[:, 1], gsend.at[:, 1], gh_send.at[1]).wait()

    @pl.when(has_prev)
    def _():
        pltpu.make_async_copy(halo.at[:, 1], halo.at[:, 1], halo_send.at[1]).wait()
        pltpu.make_async_copy(gsend.at[:, 0], gsend.at[:, 0], gh_send.at[0]).wait()


def frame_bias(slot_frames, frame_order, slab):
    frame_ids = jnp.arange(frame_order.shape[0], dtype=jnp.int32)
    one_hot = (frame_order[:, None] == frame_ids[None, :]).astype(jnp.int32)
    picked = jnp.sum(one_hot[:, :, None] * slot_frames[None, :, :], axis=1)
    hit = jnp.any(picked[None, :, :] == frame_order[:, None, None], axis=2)
    hit = hit | (frame_ids[:, None] == frame_ids[None, :])
    return jnp.repeat(jnp.where(hit, 0.0, NEGATIVE).astype(jnp.float32), slab, axis=1)


def on_device(queries, keys, values, out_grad, band_frames, frame_order):
    part, slab, columns = queries.shape
    frames = frame_order.shape[0]
    ranks = lax.axis_size("head")
    slabs = lax.axis_size("ctx")
    heads = columns // HD
    merge = math.gcd(heads // ranks, slabs)
    local_heads = heads // (ranks * merge)
    length = frames * slab
    dims = (slabs // merge, merge, ranks, local_heads, frames, part, slab)
    bias = frame_bias(band_frames[:, 0, :], frame_order, slab)
    spread = (local_heads, 4, merge * frames, slab, HD)
    edge = (local_heads, 2, 2, frames, slab, HD)
    any_spec = pl.BlockSpec(memory_space=pl.ANY)
    width = length + 2 * LANES
    outs = pl.pallas_call(
        functools.partial(kernel, dims),
        out_shape=[jax.ShapeDtypeStruct(queries.shape, queries.dtype)] * 4,
        in_specs=[any_spec] * 4 + [pl.BlockSpec(memory_space=pltpu.VMEM)],
        out_specs=[any_spec] * 4,
        scratch_shapes=[
            pltpu.VMEM(spread, jnp.bfloat16),
            pltpu.VMEM(edge, jnp.bfloat16),
            pltpu.VMEM(spread, jnp.bfloat16),
            pltpu.VMEM(edge, jnp.bfloat16),
            pltpu.VMEM(edge, jnp.bfloat16),
            pltpu.VMEM((local_heads, 2, merge * length, HD), jnp.float32),
            pltpu.VMEM((merge, frames, length), jnp.float32),
            pltpu.VMEM((merge, length, length), jnp.float32),
            pltpu.VMEM((length, length), jnp.bfloat16),
            pltpu.VMEM((length, length), jnp.bfloat16),
            pltpu.SemaphoreType.DMA,
            pltpu.SemaphoreType.DMA((local_heads,)),
            pltpu.SemaphoreType.DMA,
            pltpu.SemaphoreType.DMA((4,)),
            pltpu.SemaphoreType.DMA((2,)),
            pltpu.SemaphoreType.DMA((local_heads, 2)),
            pltpu.SemaphoreType.DMA((2,)),
            pltpu.SemaphoreType.DMA((local_heads, 2)),
            pltpu.SemaphoreType.DMA((merge,)),
            pltpu.SemaphoreType.DMA((merge,)),
        ],
        compiler_params=pltpu.CompilerParams(
            collective_id=0, has_side_effects=True, vmem_limit_bytes=50 * 1024 * 1024
        ),
        cost_estimate=pl.CostEstimate(
            flops=12 * local_heads * merge * length * width * HD,
            bytes_accessed=16 * part * slab * columns,
            transcendentals=local_heads * merge * length * width,
        ),
    )(queries, keys, values, out_grad, bias)
    return tuple(outs)


def solution(mesh):
    wide = P("head", "ctx", None)
    return jax.shard_map(
        on_device,
        mesh=mesh,
        in_specs=(wide, wide, wide, wide, P(None, "ctx", None), P()),
        out_specs=(wide,) * 4,
        check_vma=False,
    )
```

```python
import functools
import math

import jax
import jax.numpy as jnp
from jax import lax
from jax.experimental import pallas as pl
from jax.experimental.pallas import tpu as pltpu
from jax.sharding import PartitionSpec as P

HD = 128
NEGATIVE = -1e30
MESH = pl.DeviceIdType.MESH
LANES = 128


def nt(a, b):
    return lax.dot_general(a, b, (((1,), (1,)), ((), ())), preferred_element_type=jnp.float32)


def nn(a, b):
    return jnp.dot(a, b, preferred_element_type=jnp.float32)


def kernel(
    dims,
    q_ref,
    k_ref,
    v_ref,
    g_ref,
    band_hbm,
    order_hbm,
    o_ref,
    dq_ref,
    dk_ref,
    dv_ref,
    buf,
    halo,
    obuf,
    gsend,
    grecv,
    acc,
    bias_buf,
    bias_full,
    prob_t,
    grad_t,
    in_send,
    in_recv,
    out_send,
    out_recv,
    halo_send,
    halo_recv,
    gh_send,
    gh_recv,
    bias_send,
    bias_recv,
    band_ref,
    order_ref,
    band_sem,
    order_sem,
):
    groups, merge, ranks, local_heads, frames, part, slab = dims
    members = merge * ranks
    length = frames * slab
    per_chunk = LANES // slab
    scale = HD ** (-0.5)
    log_scale = scale * math.log2(math.e)

    ctx = lax.axis_index("ctx")
    rank = lax.axis_index("head")
    group = lax.div(ctx, merge)
    inner = lax.rem(ctx, merge)
    me = inner * ranks + rank
    has_prev = group > 0
    has_next = group < groups - 1
    prev_id = (ctx - merge, rank)
    next_id = (ctx + merge, rank)

    def member(step):
        slot = lax.rem(me + step, members)
        return slot, (group * merge + lax.div(slot, ranks), lax.rem(slot, ranks))

    barrier = pltpu.get_barrier_semaphore()
    for step in range(1, members):
        pl.semaphore_signal(barrier, inc=1, device_id=member(step)[1], device_id_type=MESH)

    @pl.when(has_prev)
    def _():
        pl.semaphore_signal(barrier, inc=1, device_id=prev_id, device_id_type=MESH)

    @pl.when(has_next)
    def _():
        pl.semaphore_signal(barrier, inc=1, device_id=next_id, device_id_type=MESH)

    @pl.when(jnp.logical_not(has_prev))
    def _():
        halo[:, 0] = jnp.zeros(halo.shape[:1] + halo.shape[2:], halo.dtype)

    @pl.when(jnp.logical_not(has_next))
    def _():
        halo[:, 1] = jnp.zeros(halo.shape[:1] + halo.shape[2:], halo.dtype)

    pl.semaphore_wait(
        barrier, members - 1 + has_prev.astype(jnp.int32) + has_next.astype(jnp.int32)
    )

    def bias_copy(step):
        other = lax.rem(inner + step, merge)
        return pltpu.make_async_remote_copy(
            src_ref=bias_buf.at[inner],
            dst_ref=bias_buf.at[inner],
            send_sem=bias_send.at[step],
            recv_sem=bias_recv.at[step],
            device_id=(group * merge + other, rank),
            device_id_type=MESH,
        )

    mine = pl.ds(me * part, part)

    def send_in(h):
        for step in list(range(1, members)) + [0]:
            slot, device = member(step)
            columns = pl.ds(pl.multiple_of((slot * local_heads + h) * HD, HD), HD)
            for a, source in ((1, k_ref), (2, v_ref), (0, q_ref), (3, g_ref)):
                src, dst = source.at[:, :, columns], buf.at[h, a, mine]
                if step:
                    pltpu.make_async_remote_copy(
                        src_ref=src,
                        dst_ref=dst,
                        send_sem=in_send,
                        recv_sem=in_recv.at[h],
                        device_id=device,
                        device_id_type=MESH,
                    ).start()
                else:
                    pltpu.make_async_copy(src, dst, in_recv.at[h]).start()

    send_in(0)

    band_copy = pltpu.make_async_copy(band_hbm, band_ref, band_sem)
    order_copy = pltpu.make_async_copy(order_hbm, order_ref, order_sem)
    band_copy.start()
    order_copy.start()
    band_copy.wait()
    order_copy.wait()
    row_at = lax.broadcasted_iota(jnp.int32, (frames, length), 0)
    lane_at = lax.div(lax.broadcasted_iota(jnp.int32, (frames, length), 1), slab)
    order_rows = jnp.zeros((frames, length), jnp.int32)
    for p in range(frames):
        order_rows = jnp.where(row_at == p, order_ref[p], order_rows)
    hit = row_at == lane_at
    for slot in range(band_ref.shape[1]):
        wanted = jnp.full((frames, length), -1, jnp.int32)
        for p in range(frames):
            wanted = jnp.where(lane_at == p, band_ref[0, slot, order_ref[p]], wanted)
        hit = jnp.logical_or(hit, wanted == order_rows)
    bias_buf[inner] = jnp.where(hit, 0.0, NEGATIVE)
    for step in range(1, merge):
        bias_copy(step).start()

    @pl.loop(1, local_heads)
    def _(h):
        send_in(h)

    for step in range(1, merge):
        bias_copy(step).wait()
    for s in range(merge):
        for frame in range(frames):
            bias_full[s, frame * slab : (frame + 1) * slab, :] = jnp.broadcast_to(
                bias_buf[s, frame : frame + 1, :], (slab, length)
            )

    last = (merge - 1) * frames

    def arrive(h):
        pltpu.make_async_copy(buf.at[h], buf.at[h], in_recv.at[h]).wait()

        @pl.when(has_next)
        def _():
            pltpu.make_async_remote_copy(
                src_ref=buf.at[h, pl.ds(1, 2), pl.ds(last, frames)],
                dst_ref=halo.at[h, 0],
                send_sem=halo_send.at[0],
                recv_sem=halo_recv.at[h, 0],
                device_id=next_id,
                device_id_type=MESH,
            ).start()

        @pl.when(has_prev)
        def _():
            pltpu.make_async_remote_copy(
                src_ref=buf.at[h, pl.ds(1, 2), pl.ds(0, frames)],
                dst_ref=halo.at[h, 1],
                send_sem=halo_send.at[1],
                recv_sem=halo_recv.at[h, 1],
                device_id=prev_id,
                device_id_type=MESH,
            ).start()

    def send_out(h, arrays):
        columns = pl.ds(pl.multiple_of((me * local_heads + h) * HD, HD), HD)
        for step in list(range(1, members)) + [0]:
            slot, device = member(step)
            for a, target in arrays:
                src, dst = obuf.at[h, a, pl.ds(slot * part, part)], target.at[:, :, columns]
                if step:
                    pltpu.make_async_remote_copy(
                        src_ref=src,
                        dst_ref=dst,
                        send_sem=out_send,
                        recv_sem=out_recv.at[a],
                        device_id=device,
                        device_id_type=MESH,
                    ).start()
                else:
                    pltpu.make_async_copy(src, dst, out_recv.at[a]).start()

    lane_frame = lax.div(lax.broadcasted_iota(jnp.int32, (slab, LANES), 1), slab)

    def compact(block):
        result = block[:slab]
        for i in range(1, per_chunk):
            result = jnp.where(lane_frame == i, block[i * slab : (i + 1) * slab], result)
        return result

    def expand(block):
        return jnp.concatenate(
            [jnp.where(lane_frame == i, block, 0.0) for i in range(per_chunk)], axis=0
        ).astype(jnp.bfloat16)

    def compute(h):
        @pl.when(has_prev)
        def _():
            pltpu.make_async_copy(halo.at[h, 0], halo.at[h, 0], halo_recv.at[h, 0]).wait()

        @pl.when(has_next)
        def _():
            pltpu.make_async_copy(halo.at[h, 1], halo.at[h, 1], halo_recv.at[h, 1]).wait()

        edge_prev = jnp.where(has_prev, 0.0, NEGATIVE)
        edge_next = jnp.where(has_next, 0.0, NEGATIVE)

        def rows_of(a, s):
            return buf[h, a, s * frames : (s + 1) * frames].reshape(length, HD)

        keys = [halo[h, 0, 0].reshape(length, HD)]
        values = [halo[h, 0, 1].reshape(length, HD)]
        for s in range(merge):
            keys.append(rows_of(1, s))
            values.append(rows_of(2, s))
        keys.append(halo[h, 1, 0].reshape(length, HD))
        values.append(halo[h, 1, 1].reshape(length, HD))
        keys_t = [x.T for x in keys]
        values_t = [x.T for x in values]

        acc[h] = jnp.zeros(acc.shape[1:], acc.dtype)

        def add_term(a, s, at, term):
            if s < 0 or s >= merge:
                side = 0 if s < 0 else 1
                first = at // slab
                gsend[h, side, a, first : first + per_chunk] = term.astype(jnp.bfloat16).reshape(
                    per_chunk, slab, HD
                )
            else:
                start = s * length + at
                acc[h, a, start : start + LANES] += term

        for s in range(merge):
            query, grad = rows_of(0, s), rows_of(3, s)
            own_k, own_v = keys[s + 1], values[s + 1]
            for at in range(0, length, LANES):
                rows = slice(at, at + LANES)
                q, g = query[rows], grad[rows]
                score = nt(own_k, q) * log_scale + bias_full[s, :, rows]
                score_p = compact(nt(keys[s][rows], q)) * log_scale
                score_n = compact(nt(keys[s + 2][rows], q)) * log_scale
                if s == 0:
                    score_p = score_p + edge_prev
                if s == merge - 1:
                    score_n = score_n + edge_next
                sides = jnp.maximum(score_p, score_n)
                top = jnp.maximum(
                    jnp.max(score, axis=0, keepdims=True), jnp.max(sides, axis=0, keepdims=True)
                )
                e, e_p, e_n = jnp.exp2(score - top), jnp.exp2(score_p - top), jnp.exp2(score_n - top)
                total = jnp.sum(e, axis=0, keepdims=True) + jnp.sum(
                    e_p + e_n, axis=0, keepdims=True
                )
                d = nt(own_v, g)
                d_p = compact(nt(values[s][rows], g))
                d_n = compact(nt(values[s + 2][rows], g))
                inv = 1.0 / total
                delta = inv * (
                    jnp.sum(e * d, axis=0, keepdims=True)
                    + jnp.sum(e_p * d_p + e_n * d_n, axis=0, keepdims=True)
                )
                inv_scale = inv * scale
                p = (e * inv).astype(jnp.bfloat16)
                ds = ((e * inv_scale) * (d - delta)).astype(jnp.bfloat16)
                p_p, p_n = expand(e_p * inv), expand(e_n * inv)
                ds_p = expand((e_p * inv_scale) * (d_p - delta))
                ds_n = expand((e_n * inv_scale) * (d_n - delta))
                prob_t[:, rows] = p
                grad_t[:, rows] = ds
                out_t = (
                    nn(values_t[s + 1], p)
                    + nn(values_t[s][:, rows], p_p)
                    + nn(values_t[s + 2][:, rows], p_n)
                )
                dq_t = (
                    nn(keys_t[s + 1], ds)
                    + nn(keys_t[s][:, rows], ds_p)
                    + nn(keys_t[s + 2][:, rows], ds_n)
                )
                first = s * frames + at // slab
                put = slice(first, first + per_chunk)
                obuf[h, 0, put] = out_t.T.astype(jnp.bfloat16).reshape(per_chunk, slab, HD)
                obuf[h, 1, put] = dq_t.T.astype(jnp.bfloat16).reshape(per_chunk, slab, HD)
                add_term(0, s - 1, at, nn(ds_p, q))
                add_term(1, s - 1, at, nn(p_p, g))
                add_term(0, s + 1, at, nn(ds_n, q))
                add_term(1, s + 1, at, nn(p_n, g))
            whole = slice(s * length, (s + 1) * length)
            acc[h, 0, whole] += nn(grad_t[...], query)
            acc[h, 1, whole] += nn(prob_t[...], grad)

        @pl.when(has_prev)
        def _():
            pltpu.make_async_remote_copy(
                src_ref=gsend.at[h, 0],
                dst_ref=grecv.at[h, 1],
                send_sem=gh_send.at[0],
                recv_sem=gh_recv.at[h, 1],
                device_id=prev_id,
                device_id_type=MESH,
            ).start()

        @pl.when(has_next)
        def _():
            pltpu.make_async_remote_copy(
                src_ref=gsend.at[h, 1],
                dst_ref=grecv.at[h, 0],
                send_sem=gh_send.at[1],
                recv_sem=gh_recv.at[h, 0],
                device_id=next_id,
                device_id_type=MESH,
            ).start()

        send_out(h, ((0, o_ref), (1, dq_ref)))

    def finish(h):
        for side, present, s in ((0, has_prev, 0), (1, has_next, merge - 1)):

            @pl.when(present)
            def _():
                pltpu.make_async_copy(
                    grecv.at[h, side], grecv.at[h, side], gh_recv.at[h, side]
                ).wait()
                term = grecv[h, side].astype(jnp.float32).reshape(2, length, HD)
                acc[h, :, s * length : (s + 1) * length] += term

        obuf[h, 2:4] = acc[h].astype(jnp.bfloat16).reshape(2, merge * frames, slab, HD)
        send_out(h, ((2, dk_ref), (3, dv_ref)))

    arrive(0)

    @pl.loop(0, local_heads)
    def _(h):
        @pl.when(h < local_heads - 1)
        def _():
            arrive(h + 1)

        compute(h)

        @pl.when(h > 0)
        def _():
            finish(h - 1)

    finish(local_heads - 1)

    sent = pl.ds(0, (members - 1) * part)
    pltpu.make_async_copy(buf.at[:, :, sent], buf.at[:, :, sent], in_send).wait()
    pltpu.make_async_copy(obuf.at[:, :, sent], obuf.at[:, :, sent], out_send).wait()
    for a, target in enumerate((o_ref, dq_ref, dk_ref, dv_ref)):
        pltpu.make_async_copy(target, target, out_recv.at[a]).wait()

    @pl.when(has_next)
    def _():
        pltpu.make_async_copy(halo.at[:, 0], halo.at[:, 0], halo_send.at[0]).wait()
        pltpu.make_async_copy(gsend.at[:, 1], gsend.at[:, 1], gh_send.at[1]).wait()

    @pl.when(has_prev)
    def _():
        pltpu.make_async_copy(halo.at[:, 1], halo.at[:, 1], halo_send.at[1]).wait()
        pltpu.make_async_copy(gsend.at[:, 0], gsend.at[:, 0], gh_send.at[0]).wait()


def place(*refs):
    count = (len(refs) - 3) // 2
    held, read_sem, write_sem = refs[-3:]
    reads, writes = [], []
    for i in range(count):
        src, dst = refs[i], refs[count + i]
        for j in range(src.shape[0]):
            reads.append(pltpu.make_async_copy(src.at[j], held.at[i, j], read_sem.at[i, j]))
            writes.append(pltpu.make_async_copy(held.at[i, j], dst.at[j], write_sem.at[i, j]))
    for copy in reads:
        copy.start()
    for read, write in zip(reads, writes):
        read.wait()
        write.start()
    for copy in writes:
        copy.wait()


def on_device(queries, keys, values, out_grad, band_frames, frame_order):
    part, slab, columns = queries.shape
    frames = frame_order.shape[0]
    ranks = lax.axis_size("head")
    slabs = lax.axis_size("ctx")
    heads = columns // HD
    merge = math.gcd(heads // ranks, slabs)
    local_heads = heads // (ranks * merge)
    length = frames * slab
    dims = (slabs // merge, merge, ranks, local_heads, frames, part, slab)
    spread = (local_heads, 4, merge * frames, slab, HD)
    edge = (local_heads, 2, 2, frames, slab, HD)
    any_spec = pl.BlockSpec(memory_space=pl.ANY)
    width = length + 2 * LANES
    outs = pl.pallas_call(
        functools.partial(kernel, dims),
        out_shape=[jax.ShapeDtypeStruct(queries.shape, queries.dtype)] * 4,
        in_specs=[pl.BlockSpec(memory_space=pltpu.HBM)] * 6,
        out_specs=[any_spec] * 4,
        scratch_shapes=[
            pltpu.VMEM(spread, jnp.bfloat16),
            pltpu.VMEM(edge, jnp.bfloat16),
            pltpu.VMEM(spread, jnp.bfloat16),
            pltpu.VMEM(edge, jnp.bfloat16),
            pltpu.VMEM(edge, jnp.bfloat16),
            pltpu.VMEM((local_heads, 2, merge * length, HD), jnp.float32),
            pltpu.VMEM((merge, frames, length), jnp.float32),
            pltpu.VMEM((merge, length, length), jnp.float32),
            pltpu.VMEM((length, length), jnp.bfloat16),
            pltpu.VMEM((length, length), jnp.bfloat16),
            pltpu.SemaphoreType.DMA,
            pltpu.SemaphoreType.DMA((local_heads,)),
            pltpu.SemaphoreType.DMA,
            pltpu.SemaphoreType.DMA((4,)),
            pltpu.SemaphoreType.DMA((2,)),
            pltpu.SemaphoreType.DMA((local_heads, 2)),
            pltpu.SemaphoreType.DMA((2,)),
            pltpu.SemaphoreType.DMA((local_heads, 2)),
            pltpu.SemaphoreType.DMA((merge,)),
            pltpu.SemaphoreType.DMA((merge,)),
            pltpu.SMEM((1, band_frames.shape[2], frames), jnp.int32),
            pltpu.SMEM((frames,), jnp.int32),
            pltpu.SemaphoreType.DMA,
            pltpu.SemaphoreType.DMA,
        ],
        compiler_params=pltpu.CompilerParams(
            collective_id=0, has_side_effects=True, vmem_limit_bytes=58 * 1024 * 1024
        ),
        cost_estimate=pl.CostEstimate(
            flops=12 * local_heads * merge * length * width * HD,
            bytes_accessed=16 * part * slab * columns,
            transcendentals=local_heads * merge * length * width,
        ),
    )(queries, keys, values, out_grad, jnp.transpose(band_frames, (1, 2, 0)), frame_order)
    placed = pl.pallas_call(
        place,
        out_shape=[jax.ShapeDtypeStruct(x.shape, x.dtype) for x in outs],
        in_specs=[pl.BlockSpec(memory_space=pltpu.HBM)] * 4,
        out_specs=[pl.BlockSpec(memory_space=pltpu.HBM)] * 4,
        scratch_shapes=[
            pltpu.VMEM((4, part, slab, columns), queries.dtype),
            pltpu.SemaphoreType.DMA((4, part)),
            pltpu.SemaphoreType.DMA((4, part)),
        ],
        compiler_params=pltpu.CompilerParams(vmem_limit_bytes=58 * 1024 * 1024),
    )(*outs)
    return tuple(placed)


def solution(mesh):
    wide = P("head", "ctx", None)
    return jax.shard_map(
        on_device,
        mesh=mesh,
        in_specs=(wide, wide, wide, wide, P(None, "ctx", None), P()),
        out_specs=(wide,) * 4,
        check_vma=False,
    )
```

```python
import functools
import math

import jax
import jax.numpy as jnp
from jax import lax
from jax.experimental import pallas as pl
from jax.experimental.pallas import tpu as pltpu
from jax.sharding import PartitionSpec as P

HD = 128
NEGATIVE = -1e30
MESH = pl.DeviceIdType.MESH
LANES = 128


def nt(a, b):
    return lax.dot_general(a, b, (((1,), (1,)), ((), ())), preferred_element_type=jnp.float32)


def nn(a, b):
    return jnp.dot(a, b, preferred_element_type=jnp.float32)


def kernel(
    dims,
    q_ref,
    k_ref,
    v_ref,
    g_ref,
    band_hbm,
    order_hbm,
    o_ref,
    dq_ref,
    dk_ref,
    dv_ref,
    buf,
    halo,
    obuf,
    gsend,
    grecv,
    acc,
    bias_buf,
    bias_full,
    prob_t,
    grad_t,
    in_send,
    in_recv,
    out_send,
    out_recv,
    halo_send,
    halo_recv,
    gh_send,
    gh_recv,
    bias_send,
    bias_recv,
    band_ref,
    order_ref,
    band_sem,
    order_sem,
):
    groups, merge, ranks, local_heads, frames, part, slab = dims
    members = merge * ranks
    length = frames * slab
    per_chunk = LANES // slab
    scale = HD ** (-0.5)
    log_scale = scale * math.log2(math.e)

    ctx = lax.axis_index("ctx")
    rank = lax.axis_index("head")
    group = lax.div(ctx, merge)
    inner = lax.rem(ctx, merge)
    me = inner * ranks + rank
    has_prev = group > 0
    has_next = group < groups - 1
    prev_id = (ctx - merge, rank)
    next_id = (ctx + merge, rank)

    def member(step):
        slot = lax.rem(me + step, members)
        return slot, (group * merge + lax.div(slot, ranks), lax.rem(slot, ranks))

    barrier = pltpu.get_barrier_semaphore()
    for step in range(1, members):
        pl.semaphore_signal(barrier, inc=1, device_id=member(step)[1], device_id_type=MESH)

    @pl.when(has_prev)
    def _():
        pl.semaphore_signal(barrier, inc=1, device_id=prev_id, device_id_type=MESH)

    @pl.when(has_next)
    def _():
        pl.semaphore_signal(barrier, inc=1, device_id=next_id, device_id_type=MESH)

    @pl.when(jnp.logical_not(has_prev))
    def _():
        halo[:, 0] = jnp.zeros(halo.shape[:1] + halo.shape[2:], halo.dtype)

    @pl.when(jnp.logical_not(has_next))
    def _():
        halo[:, 1] = jnp.zeros(halo.shape[:1] + halo.shape[2:], halo.dtype)

    pl.semaphore_wait(
        barrier, members - 1 + has_prev.astype(jnp.int32) + has_next.astype(jnp.int32)
    )

    def bias_copy(step):
        other = lax.rem(inner + step, merge)
        return pltpu.make_async_remote_copy(
            src_ref=bias_buf.at[inner],
            dst_ref=bias_buf.at[inner],
            send_sem=bias_send.at[step],
            recv_sem=bias_recv.at[step],
            device_id=(group * merge + other, rank),
            device_id_type=MESH,
        )

    mine = pl.ds(me * part, part)

    def send_in(h):
        for step in list(range(1, members)) + [0]:
            slot, device = member(step)
            columns = pl.ds(pl.multiple_of((slot * local_heads + h) * HD, HD), HD)
            for a, source in ((1, k_ref), (2, v_ref), (0, q_ref), (3, g_ref)):
                src, dst = source.at[:, :, columns], buf.at[h, a, mine]
                if step:
                    pltpu.make_async_remote_copy(
                        src_ref=src,
                        dst_ref=dst,
                        send_sem=in_send,
                        recv_sem=in_recv.at[h],
                        device_id=device,
                        device_id_type=MESH,
                    ).start()
                else:
                    pltpu.make_async_copy(src, dst, in_recv.at[h]).start()

    send_in(0)

    band_copy = pltpu.make_async_copy(band_hbm, band_ref, band_sem)
    order_copy = pltpu.make_async_copy(order_hbm, order_ref, order_sem)
    band_copy.start()
    order_copy.start()
    band_copy.wait()
    order_copy.wait()
    row_at = lax.broadcasted_iota(jnp.int32, (frames, length), 0)
    lane_at = lax.div(lax.broadcasted_iota(jnp.int32, (frames, length), 1), slab)
    order_rows = jnp.zeros((frames, length), jnp.int32)
    for p in range(frames):
        order_rows = jnp.where(row_at == p, order_ref[p], order_rows)
    hit = row_at == lane_at
    for slot in range(band_ref.shape[1]):
        wanted = jnp.full((frames, length), -1, jnp.int32)
        for p in range(frames):
            wanted = jnp.where(lane_at == p, band_ref[0, slot, order_ref[p]], wanted)
        hit = jnp.logical_or(hit, wanted == order_rows)
    bias_buf[inner] = jnp.where(hit, 0.0, NEGATIVE)
    for step in range(1, merge):
        bias_copy(step).start()

    @pl.loop(1, local_heads)
    def _(h):
        send_in(h)

    for step in range(1, merge):
        bias_copy(step).wait()
    for s in range(merge):
        for frame in range(frames):
            bias_full[s, frame * slab : (frame + 1) * slab, :] = jnp.broadcast_to(
                bias_buf[s, frame : frame + 1, :], (slab, length)
            )

    last = (merge - 1) * frames

    def arrive(h):
        pltpu.make_async_copy(buf.at[h], buf.at[h], in_recv.at[h]).wait()

        @pl.when(has_next)
        def _():
            pltpu.make_async_remote_copy(
                src_ref=buf.at[h, pl.ds(1, 2), pl.ds(last, frames)],
                dst_ref=halo.at[h, 0],
                send_sem=halo_send.at[0],
                recv_sem=halo_recv.at[h, 0],
                device_id=next_id,
                device_id_type=MESH,
            ).start()

        @pl.when(has_prev)
        def _():
            pltpu.make_async_remote_copy(
                src_ref=buf.at[h, pl.ds(1, 2), pl.ds(0, frames)],
                dst_ref=halo.at[h, 1],
                send_sem=halo_send.at[1],
                recv_sem=halo_recv.at[h, 1],
                device_id=prev_id,
                device_id_type=MESH,
            ).start()

    def send_out(h, arrays):
        columns = pl.ds(pl.multiple_of((me * local_heads + h) * HD, HD), HD)
        for step in list(range(1, members)) + [0]:
            slot, device = member(step)
            for a, target in arrays:
                src, dst = obuf.at[h, a, pl.ds(slot * part, part)], target.at[:, :, columns]
                if step:
                    pltpu.make_async_remote_copy(
                        src_ref=src,
                        dst_ref=dst,
                        send_sem=out_send,
                        recv_sem=out_recv.at[a],
                        device_id=device,
                        device_id_type=MESH,
                    ).start()
                else:
                    pltpu.make_async_copy(src, dst, out_recv.at[a]).start()

    lane_frame = lax.div(lax.broadcasted_iota(jnp.int32, (slab, LANES), 1), slab)

    def compact(block):
        result = block[:slab]
        for i in range(1, per_chunk):
            result = jnp.where(lane_frame == i, block[i * slab : (i + 1) * slab], result)
        return result

    def expand(block):
        return jnp.concatenate(
            [jnp.where(lane_frame == i, block, 0.0) for i in range(per_chunk)], axis=0
        ).astype(jnp.bfloat16)

    def compute(h):
        @pl.when(has_prev)
        def _():
            pltpu.make_async_copy(halo.at[h, 0], halo.at[h, 0], halo_recv.at[h, 0]).wait()

        @pl.when(has_next)
        def _():
            pltpu.make_async_copy(halo.at[h, 1], halo.at[h, 1], halo_recv.at[h, 1]).wait()

        edge_prev = jnp.where(has_prev, 0.0, NEGATIVE)
        edge_next = jnp.where(has_next, 0.0, NEGATIVE)

        def rows_of(a, s):
            return buf[h, a, s * frames : (s + 1) * frames].reshape(length, HD)

        keys = [halo[h, 0, 0].reshape(length, HD)]
        values = [halo[h, 0, 1].reshape(length, HD)]
        for s in range(merge):
            keys.append(rows_of(1, s))
            values.append(rows_of(2, s))
        keys.append(halo[h, 1, 0].reshape(length, HD))
        values.append(halo[h, 1, 1].reshape(length, HD))
        keys_t = [x.T for x in keys]
        values_t = [x.T for x in values]

        acc[h] = jnp.zeros(acc.shape[1:], acc.dtype)

        def add_term(a, s, at, term):
            if s < 0 or s >= merge:
                side = 0 if s < 0 else 1
                first = at // slab
                gsend[h, side, a, first : first + per_chunk] = term.astype(jnp.bfloat16).reshape(
                    per_chunk, slab, HD
                )
            else:
                start = s * length + at
                acc[h, a, start : start + LANES] += term

        for s in range(merge):
            query, grad = rows_of(0, s), rows_of(3, s)
            own_k, own_v = keys[s + 1], values[s + 1]
            for at in range(0, length, LANES):
                rows = slice(at, at + LANES)
                q, g = query[rows], grad[rows]
                score = nt(own_k, q) * log_scale + bias_full[s, :, rows]
                score_p = compact(nt(keys[s][rows], q)) * log_scale
                score_n = compact(nt(keys[s + 2][rows], q)) * log_scale
                if s == 0:
                    score_p = score_p + edge_prev
                if s == merge - 1:
                    score_n = score_n + edge_next
                sides = jnp.maximum(score_p, score_n)
                top = jnp.maximum(
                    jnp.max(score, axis=0, keepdims=True), jnp.max(sides, axis=0, keepdims=True)
                )
                e, e_p, e_n = jnp.exp2(score - top), jnp.exp2(score_p - top), jnp.exp2(score_n - top)
                total = jnp.sum(e, axis=0, keepdims=True) + jnp.sum(
                    e_p + e_n, axis=0, keepdims=True
                )
                d = nt(own_v, g)
                d_p = compact(nt(values[s][rows], g))
                d_n = compact(nt(values[s + 2][rows], g))
                inv = 1.0 / total
                delta = inv * (
                    jnp.sum(e * d, axis=0, keepdims=True)
                    + jnp.sum(e_p * d_p + e_n * d_n, axis=0, keepdims=True)
                )
                inv_scale = inv * scale
                p = (e * inv).astype(jnp.bfloat16)
                ds = ((e * inv_scale) * (d - delta)).astype(jnp.bfloat16)
                p_p, p_n = expand(e_p * inv), expand(e_n * inv)
                ds_p = expand((e_p * inv_scale) * (d_p - delta))
                ds_n = expand((e_n * inv_scale) * (d_n - delta))
                prob_t[:, rows] = p
                grad_t[:, rows] = ds
                out_t = (
                    nn(values_t[s + 1], p)
                    + nn(values_t[s][:, rows], p_p)
                    + nn(values_t[s + 2][:, rows], p_n)
                )
                dq_t = (
                    nn(keys_t[s + 1], ds)
                    + nn(keys_t[s][:, rows], ds_p)
                    + nn(keys_t[s + 2][:, rows], ds_n)
                )
                first = s * frames + at // slab
                put = slice(first, first + per_chunk)
                obuf[h, 0, put] = out_t.T.astype(jnp.bfloat16).reshape(per_chunk, slab, HD)
                obuf[h, 1, put] = dq_t.T.astype(jnp.bfloat16).reshape(per_chunk, slab, HD)
                add_term(0, s - 1, at, nn(ds_p, q))
                add_term(1, s - 1, at, nn(p_p, g))
                add_term(0, s + 1, at, nn(ds_n, q))
                add_term(1, s + 1, at, nn(p_n, g))
            whole = slice(s * length, (s + 1) * length)
            acc[h, 0, whole] += nn(grad_t[...], query)
            acc[h, 1, whole] += nn(prob_t[...], grad)

        @pl.when(has_prev)
        def _():
            pltpu.make_async_remote_copy(
                src_ref=gsend.at[h, 0],
                dst_ref=grecv.at[h, 1],
                send_sem=gh_send.at[0],
                recv_sem=gh_recv.at[h, 1],
                device_id=prev_id,
                device_id_type=MESH,
            ).start()

        @pl.when(has_next)
        def _():
            pltpu.make_async_remote_copy(
                src_ref=gsend.at[h, 1],
                dst_ref=grecv.at[h, 0],
                send_sem=gh_send.at[1],
                recv_sem=gh_recv.at[h, 0],
                device_id=next_id,
                device_id_type=MESH,
            ).start()

        send_out(h, ((0, o_ref), (1, dq_ref)))

    def finish(h):
        for side, present, s in ((0, has_prev, 0), (1, has_next, merge - 1)):

            @pl.when(present)
            def _():
                pltpu.make_async_copy(
                    grecv.at[h, side], grecv.at[h, side], gh_recv.at[h, side]
                ).wait()
                term = grecv[h, side].astype(jnp.float32).reshape(2, length, HD)
                acc[h, :, s * length : (s + 1) * length] += term

        obuf[h, 2:4] = acc[h].astype(jnp.bfloat16).reshape(2, merge * frames, slab, HD)
        send_out(h, ((2, dk_ref), (3, dv_ref)))

    arrive(0)

    @pl.loop(0, local_heads)
    def _(h):
        @pl.when(h < local_heads - 1)
        def _():
            arrive(h + 1)

        compute(h)

        @pl.when(h > 0)
        def _():
            finish(h - 1)

    finish(local_heads - 1)

    sent = pl.ds(0, (members - 1) * part)
    pltpu.make_async_copy(buf.at[:, :, sent], buf.at[:, :, sent], in_send).wait()
    pltpu.make_async_copy(obuf.at[:, :, sent], obuf.at[:, :, sent], out_send).wait()
    for a, target in enumerate((o_ref, dq_ref, dk_ref, dv_ref)):
        pltpu.make_async_copy(target, target, out_recv.at[a]).wait()

    @pl.when(has_next)
    def _():
        pltpu.make_async_copy(halo.at[:, 0], halo.at[:, 0], halo_send.at[0]).wait()
        pltpu.make_async_copy(gsend.at[:, 1], gsend.at[:, 1], gh_send.at[1]).wait()

    @pl.when(has_prev)
    def _():
        pltpu.make_async_copy(halo.at[:, 1], halo.at[:, 1], halo_send.at[1]).wait()
        pltpu.make_async_copy(gsend.at[:, 0], gsend.at[:, 0], gh_send.at[0]).wait()


def place(*refs):
    count = (len(refs) - 1) // 2
    sems = refs[-1]
    copies = []
    for i in range(count):
        src, dst = refs[i], refs[count + i]
        for j in range(src.shape[0]):
            copies.append(pltpu.make_async_copy(src.at[j], dst.at[j], sems.at[i, j]))
    for copy in copies:
        copy.start()
    for copy in copies:
        copy.wait()


def on_device(queries, keys, values, out_grad, band_frames, frame_order):
    part, slab, columns = queries.shape
    frames = frame_order.shape[0]
    ranks = lax.axis_size("head")
    slabs = lax.axis_size("ctx")
    heads = columns // HD
    merge = math.gcd(heads // ranks, slabs)
    local_heads = heads // (ranks * merge)
    length = frames * slab
    dims = (slabs // merge, merge, ranks, local_heads, frames, part, slab)
    spread = (local_heads, 4, merge * frames, slab, HD)
    edge = (local_heads, 2, 2, frames, slab, HD)
    any_spec = pl.BlockSpec(memory_space=pl.ANY)
    width = length + 2 * LANES
    outs = pl.pallas_call(
        functools.partial(kernel, dims),
        out_shape=[jax.ShapeDtypeStruct(queries.shape, queries.dtype)] * 4,
        in_specs=[pl.BlockSpec(memory_space=pltpu.HBM)] * 6,
        out_specs=[any_spec] * 4,
        scratch_shapes=[
            pltpu.VMEM(spread, jnp.bfloat16),
            pltpu.VMEM(edge, jnp.bfloat16),
            pltpu.VMEM(spread, jnp.bfloat16),
            pltpu.VMEM(edge, jnp.bfloat16),
            pltpu.VMEM(edge, jnp.bfloat16),
            pltpu.VMEM((local_heads, 2, merge * length, HD), jnp.float32),
            pltpu.VMEM((merge, frames, length), jnp.float32),
            pltpu.VMEM((merge, length, length), jnp.float32),
            pltpu.VMEM((length, length), jnp.bfloat16),
            pltpu.VMEM((length, length), jnp.bfloat16),
            pltpu.SemaphoreType.DMA,
            pltpu.SemaphoreType.DMA((local_heads,)),
            pltpu.SemaphoreType.DMA,
            pltpu.SemaphoreType.DMA((4,)),
            pltpu.SemaphoreType.DMA((2,)),
            pltpu.SemaphoreType.DMA((local_heads, 2)),
            pltpu.SemaphoreType.DMA((2,)),
            pltpu.SemaphoreType.DMA((local_heads, 2)),
            pltpu.SemaphoreType.DMA((merge,)),
            pltpu.SemaphoreType.DMA((merge,)),
            pltpu.SMEM((1, band_frames.shape[2], frames), jnp.int32),
            pltpu.SMEM((frames,), jnp.int32),
            pltpu.SemaphoreType.DMA,
            pltpu.SemaphoreType.DMA,
        ],
        compiler_params=pltpu.CompilerParams(
            collective_id=0, has_side_effects=True, vmem_limit_bytes=48 * 1024 * 1024
        ),
        cost_estimate=pl.CostEstimate(
            flops=12 * local_heads * merge * length * width * HD,
            bytes_accessed=16 * part * slab * columns,
            transcendentals=local_heads * merge * length * width,
        ),
    )(queries, keys, values, out_grad, jnp.transpose(band_frames, (1, 2, 0)), frame_order)
    placed = pl.pallas_call(
        place,
        out_shape=[jax.ShapeDtypeStruct(x.shape, x.dtype) for x in outs],
        in_specs=[pl.BlockSpec(memory_space=pltpu.VMEM)] * 4,
        out_specs=[pl.BlockSpec(memory_space=pltpu.HBM)] * 4,
        scratch_shapes=[pltpu.SemaphoreType.DMA((4, part))],
        compiler_params=pltpu.CompilerParams(vmem_limit_bytes=8 * 1024 * 1024),
    )(*outs)
    return tuple(placed)


def solution(mesh):
    wide = P("head", "ctx", None)
    return jax.shard_map(
        on_device,
        mesh=mesh,
        in_specs=(wide, wide, wide, wide, P(None, "ctx", None), P()),
        out_specs=(wide,) * 4,
        check_vma=False,
    )
```
